256 devices in a mesh: dp: 4 (over x_lo, core), blk: 64 (over x_hi, z, y).
Axes of the slice: x: 4 (x_hi: 2, x_lo: 2; x = x_hi * 2 + x_lo), y: 4, z: 8, core: 2. Of those that a mesh axis runs over, the one named last changes fastest.
Arguments:
- tokens: bfloat16 [65536, 3072], P(('dp', 'blk')), may hold values from -6 to 6
- cotangent: bfloat16 [65536, 3072], P(('dp', 'blk')), may hold values from -6 to 6
- norm_gain: float32 [3072], replicated, may hold values from 0.1 to 1.9
- gate_weight: bfloat16 [3072, 8192], P(None, 'blk'), may hold values from -0.109375 to 0.109375
- up_weight: bfloat16 [3072, 8192], P(None, 'blk'), may hold values from -0.109375 to 0.109375
- down_weight: bfloat16 [8192, 3072], P('blk'), may hold values from -0.0625 to 0.0625
Outputs:
- block_out: bfloat16 [65536, 3072], P(('dp', 'blk'))
- input_grad: bfloat16 [65536, 3072], P(('dp', 'blk'))
- gate_grad: float32 [3072, 8192], P('dp', 'blk')
- up_grad: float32 [3072, 8192], P('dp', 'blk')
- down_grad: float32 [8192, 3072], P('blk', 'dp')
The draws below stay inside these ranges and needn't reach their ends.
All inputs are finite; a program needn't handle non-finite values.
Results may differ from the reference program's by a relative error of at most 0.006.
Values may be sent and summed in bfloat16 or wider, within the bound.
No kernel may reach another device: no remote copies, remote signals or barrier semaphores. Data moves between devices by JAX's collectives and lax.ppermute only.
A program may use at most 128 MiB of HBM per device.

```python
import jax
import jax.numpy as jnp
from jax import lax

D = 3072
HID = 128
ROWS = 256
HOPS = 3
FF = 8192
TOKENS = 65536
N_DP = 4
N_BLK = 64


def shard_levels(own_key, shape, pieces, least, high):
    gain = 1.0
    for dim, blocks in pieces:
        heights = jax.random.uniform(jax.random.fold_in(jax.random.fold_in(own_key, 6), dim), (blocks,), jnp.float32, least / len(pieces), high / len(pieces))
        gain = gain * jnp.repeat(jnp.exp(heights), shape[dim] // blocks).reshape((-1,) + (1,) * (len(shape) - 1 - dim))
    return gain


def scatter_about(own_key, extent, spread, limit, pieces=(), held_as=jnp.bfloat16):
    gain = shard_levels(own_key, extent, pieces, -0.22, 0.18) if pieces else 1.0
    drawn = jax.random.normal(own_key, extent, jnp.float32) * spread * gain
    return jnp.minimum(jnp.maximum(drawn, -limit), limit).astype(held_as)


def setup_inputs(seed: int = 0) -> dict:
    keys = jax.random.split(jax.random.key(seed), 7)
    return {
        "tokens": scatter_about(keys[0], (TOKENS, D), 1.0, 6.0, ((0, 256),)),
        "cotangent": scatter_about(keys[1], (TOKENS, D), 1.0, 6.0, ((0, 256),)),
        "norm_gain": jnp.clip(1.0 + 0.18 * jax.random.normal(keys[2], (D,), jnp.float32), 0.1, 1.9),
        "gate_weight": scatter_about(keys[3], (D, FF), D ** -0.5, 0.109375, ((1, 64),)),
        "up_weight": scatter_about(keys[4], (D, FF), D ** -0.5, 0.109375, ((1, 64),)),
        "down_weight": scatter_about(keys[5], (FF, D), FF ** -0.5, 0.0625, ((0, 64),)),
    }


epsilon = 1e-05
grad_scale = 0.0625

def rounded(value):
    narrow = lax.optimization_barrier(value.astype(jnp.bfloat16))
    return narrow.astype(jnp.float32)

def reference(tokens, cotangent, norm_gain, gate_weight, up_weight, down_weight):
    cycle = N_BLK
    token_blocks = tokens.reshape(N_DP, cycle, ROWS, D)
    cot_blocks = cotangent.reshape(N_DP, cycle, ROWS, D)
    gate_spans = gate_weight.astype(jnp.float32).reshape(D, cycle, HID)
    up_spans = up_weight.astype(jnp.float32).reshape(D, cycle, HID)
    down_spans = down_weight.astype(jnp.float32).reshape(cycle, HID, D)

    def window(pair):
        block, cot = pair
        wide = block.astype(jnp.float32)
        cot_wide = cot.astype(jnp.float32)
        inverse = lax.rsqrt(lax.optimization_barrier(jnp.mean(wide * wide, axis=-1, keepdims=True)) + epsilon)
        normed = rounded(wide * inverse * norm_gain)
        mlp_total = jnp.zeros((cycle, ROWS, D), jnp.float32)
        dnormed = jnp.zeros((cycle, ROWS, D), jnp.float32)
        gate_acc = jnp.zeros((cycle, D, HID), jnp.float32)
        up_acc = jnp.zeros((cycle, D, HID), jnp.float32)
        down_acc = jnp.zeros((cycle, HID, D), jnp.float32)
        for hop_index in range(HOPS):
            gate_part = jnp.roll(gate_spans, hop_index, axis=1)
            up_part = jnp.roll(up_spans, hop_index, axis=1)
            down_part = jnp.roll(down_spans, hop_index, axis=0)
            pre_gate = jnp.einsum('brd,dbh->brh', normed, gate_part)
            pre_up = jnp.einsum('brd,dbh->brh', normed, up_part)
            sigmoid_gate = jax.nn.sigmoid(pre_gate)
            active = pre_gate * sigmoid_gate
            hidden = rounded(active * pre_up)
            mlp_total = mlp_total + jnp.einsum('brh,bhd->brd', hidden, down_part)
            hidden_grad = jnp.einsum('brd,bhd->brh', cot_wide, down_part)
            gate_delta = rounded(hidden_grad * pre_up * sigmoid_gate * (1.0 + pre_gate * (1.0 - sigmoid_gate)))
            up_delta = rounded(hidden_grad * active)
            dnormed = dnormed + jnp.einsum('brh,dbh->brd', gate_delta, gate_part) + jnp.einsum('brh,dbh->brd', up_delta, up_part)
            gate_term = jnp.einsum('brd,brh->bdh', normed, gate_delta)
            up_term = jnp.einsum('brd,brh->bdh', normed, up_delta)
            down_term = jnp.einsum('brh,brd->bhd', hidden, cot_wide)
            gate_acc = gate_acc + jnp.roll(gate_term, -hop_index, axis=0)
            up_acc = up_acc + jnp.roll(up_term, -hop_index, axis=0)
            down_acc = down_acc + jnp.roll(down_term, -hop_index, axis=0)
        block_out = (wide + mlp_total).astype(jnp.bfloat16)
        scaled = wide * inverse
        along = dnormed * norm_gain
        norm_back = inverse * (along - scaled * lax.optimization_barrier(jnp.mean(along * scaled, axis=-1, keepdims=True)))
        input_grad = (cot_wide + norm_back).astype(jnp.bfloat16)
        return (block_out, input_grad, gate_acc, up_acc, down_acc)
    results = lax.map(window, (token_blocks, cot_blocks))
    block_out = results[0].reshape(TOKENS, D)
    input_grad = results[1].reshape(TOKENS, D)
    gate_grad = jnp.transpose(lax.optimization_barrier(jnp.sum(results[2], axis=0)), (1, 0, 2)).reshape(D, FF) * grad_scale
    up_grad = jnp.transpose(lax.optimization_barrier(jnp.sum(results[3], axis=0)), (1, 0, 2)).reshape(D, FF) * grad_scale
    down_grad = lax.optimization_barrier(jnp.sum(results[4], axis=0)).reshape(FF, D) * grad_scale
    return (block_out, input_grad, gate_grad, up_grad, down_grad)
```

```python
import jax
import jax.numpy as jnp
from jax import lax
from jax.sharding import PartitionSpec as P

HOPS = 3
DP = 4


epsilon = 1e-05
grad_scale = 0.0625


def from_behind(value, steps):
    count = lax.axis_size("blk")
    pairs = [(source, (source + steps) % count) for source in range(count)]
    return lax.ppermute(value, "blk", pairs)


def swap(value, bit):
    return lax.ppermute(value, "dp", [(source, source ^ bit) for source in range(DP)])


def wire(value):
    return value.astype(jnp.bfloat16)


def relative_columns(value, place):
    width = value.shape[1] // DP
    blocks = [
        lax.dynamic_slice_in_dim(value, (place ^ k) * width, width, axis=1) for k in range(DP)
    ]
    return jnp.concatenate(blocks, axis=1)


def relative_rows(value, place):
    height = value.shape[0] // DP
    blocks = [
        lax.dynamic_slice_in_dim(value, (place ^ k) * height, height, axis=0) for k in range(DP)
    ]
    return jnp.concatenate(blocks, axis=0)


def shards(tokens, cotangent, norm_gain, gate_weight, up_weight, down_weight):
    contract_rows = (((0,), (0,)), ((), ()))
    contract_cols = (((1,), (1,)), ((), ()))
    place = lax.axis_index("dp")
    model = tokens.shape[1]
    part = model // DP
    units = gate_weight.shape[1]

    quarter = jnp.concatenate(
        [
            lax.dynamic_slice_in_dim(gate_weight, place * part, part, axis=0),
            lax.dynamic_slice_in_dim(up_weight, place * part, part, axis=0),
            jnp.transpose(lax.dynamic_slice_in_dim(down_weight, place * part, part, axis=1)),
        ],
        axis=1,
    )
    first = from_behind(quarter, 1)
    second = from_behind(first, 1)

    def whole(piece):
        half = jnp.concatenate([piece, swap(piece, 2)], axis=0)
        return half, swap(half, 1)

    wide = tokens.astype(jnp.float32)
    inverse = lax.rsqrt(jnp.mean(wide * wide, axis=-1, keepdims=True) + epsilon)
    normed = (wide * inverse * norm_gain).astype(jnp.bfloat16)
    normed_rel = relative_columns(normed, place)
    cot_rel = relative_columns(cotangent, place)

    def order(value):
        cut = [value[:, k * part:(k + 1) * part] for k in range(DP)]
        return (
            jnp.concatenate([cut[0], cut[2]], axis=1),
            jnp.concatenate([cut[1], cut[3]], axis=1),
        )

    normed_near, normed_far = order(normed_rel)
    cot_near, cot_far = order(cot_rel)

    own_rel = relative_rows(
        jnp.concatenate([gate_weight, up_weight, jnp.transpose(down_weight)], axis=1), place
    )
    own = (
        jnp.concatenate([own_rel[:part], own_rel[2 * part:3 * part]], axis=0),
        jnp.concatenate([own_rel[part:2 * part], own_rel[3 * part:]], axis=0),
    )
    held = [own, whole(first), whole(second)]

    hidden_all = []
    delta_all = []
    sums = []
    for near, far in held:
        pre = jnp.dot(normed_near, near[:, :2 * units], preferred_element_type=jnp.float32)
        pre = pre + jnp.dot(normed_far, far[:, :2 * units], preferred_element_type=jnp.float32)
        hidden_grad = jnp.dot(cot_near, near[:, 2 * units:], preferred_element_type=jnp.float32)
        hidden_grad = hidden_grad + jnp.dot(
            cot_far, far[:, 2 * units:], preferred_element_type=jnp.float32
        )
        pre_gate, pre_up = pre[:, :units], pre[:, units:]
        sigmoid_gate = jax.nn.sigmoid(pre_gate)
        active = pre_gate * sigmoid_gate
        hidden = (active * pre_up).astype(jnp.bfloat16)
        gate_delta = (
            hidden_grad * pre_up * sigmoid_gate * (1.0 + pre_gate * (1.0 - sigmoid_gate))
        ).astype(jnp.bfloat16)
        up_delta = (hidden_grad * active).astype(jnp.bfloat16)
        delta = jnp.concatenate([gate_delta, up_delta], axis=1)
        hidden_all.append(hidden)
        delta_all.append(delta)

        def terms(normed_half, cot_half):
            return jnp.concatenate(
                [
                    lax.dot_general(
                        normed_half, delta, contract_rows, preferred_element_type=jnp.float32
                    ),
                    lax.dot_general(
                        cot_half, hidden, contract_rows, preferred_element_type=jnp.float32
                    ),
                ],
                axis=1,
            )

        arrived = swap(wire(terms(normed_far, cot_far)), 1)
        chip = terms(normed_near, cot_near) + arrived
        arrived = swap(wire(chip[part:]), 2)
        sums.append(chip[:part] + arrived)

    hidden = jnp.concatenate(hidden_all, axis=1)
    delta = jnp.concatenate(delta_all, axis=1)

    def outward(value, start, stop):
        halves = []
        for side in range(2):
            weights = jnp.concatenate([pair[side][:, start:stop] for pair in held], axis=1)
            halves.append(
                lax.dot_general(value, weights, contract_cols, preferred_element_type=jnp.float32)
            )
        near, far = halves
        rel = jnp.concatenate(
            [near[:, :part], far[:, :part], near[:, part:], far[:, part:]], axis=1
        )
        return relative_columns(rel, place)

    mlp_total = outward(hidden, 2 * units, 3 * units)
    dnormed = outward(delta, 0, 2 * units)
    block_out = (wide + mlp_total).astype(jnp.bfloat16)
    scaled = wide * inverse
    along = dnormed * norm_gain
    norm_back = inverse * (along - scaled * jnp.mean(along * scaled, axis=-1, keepdims=True))
    input_grad = (cotangent.astype(jnp.float32) + norm_back).astype(jnp.bfloat16)

    carried = sums[2]
    carried = from_behind(wire(carried), -1) + sums[1]
    carried = from_behind(wire(carried), -1) + sums[0]
    carried = carried * grad_scale
    return (
        block_out,
        input_grad,
        carried[:, :units],
        carried[:, units:2 * units],
        jnp.transpose(carried[:, 2 * units:]),
    )


def solution(mesh):
    in_specs = (
        P(("dp", "blk"), None),
        P(("dp", "blk"), None),
        P(),
        P(None, "blk"),
        P(None, "blk"),
        P("blk", None),
    )
    out_specs = (
        P(("dp", "blk"), None),
        P(("dp", "blk"), None),
        P("dp", "blk"),
        P("dp", "blk"),
        P("blk", "dp"),
    )
    return jax.shard_map(shards, mesh=mesh, in_specs=in_specs, out_specs=out_specs, check_vma=False)
```

```python
import functools

import jax
import jax.numpy as jnp
from jax import lax
from jax.experimental import pallas as pl
from jax.experimental.pallas import tpu as pltpu
from jax.sharding import PartitionSpec as P

DP = 4
RING = 4
TIE_LIMIT = 1024 * 1024
VMEM_LIMIT = 12 * 1024 * 1024


epsilon = 1e-05
grad_scale = 0.0625

BOTH = ("dp", "blk")
NN = (((1,), (0,)), ((), ()))
FLAG = ((8, 128), jnp.float32)
NT = (((1,), (1,)), ((), ()))
TN = (((0,), (0,)), ((), ()))
STRIP = 16


def mul(left, right, dims=NN):
    return lax.dot_general(left, right, dims, preferred_element_type=jnp.float32)


def move(value, target):
    count = lax.axis_size("blk")
    pairs = []
    for place in range(DP):
        for block in range(count):
            to_place, to_block = target(place, block)
            pairs.append((place * count + block, to_place * count + to_block % count))
    return lax.ppermute(value, BOTH, pairs)


def swap(value, bit):
    return lax.ppermute(value, "dp", [(source, source ^ bit) for source in range(DP)])


def turn(block, step):
    return block // RING * RING + (block + step) % RING


def half_of(count):
    return count // 2


def forward(value):
    def target(place, block):
        half = half_of(lax.axis_size("blk"))
        return place ^ (2 if block % half == half - 1 else 0), block + 1

    return move(value, target)


def backward(value):
    def target(place, block):
        half = half_of(lax.axis_size("blk"))
        return place ^ (2 if block % half == 0 else 0), block - 1

    return move(value, target)


def back_two(value):
    def target(place, block):
        half = half_of(lax.axis_size("blk"))
        return place ^ (2 if block % half < 2 else 0), block - 2

    return move(value, target)


def around_first(value):
    return move(value, lambda place, block: (place, turn(block, -1)))


def around_second(value):
    def target(place, block):
        half = half_of(lax.axis_size("blk"))
        source = turn(block, 1)
        return place ^ (2 if source % half >= half - 2 else 0), source + 2

    return move(value, target)


def call(kernel, operands, shapes, micros, far=(), tokens=(), scalars=(), scratch=(), direct=False, flag=False):
    whole = pl.BlockSpec(memory_space=pltpu.VMEM)
    anywhere = pl.BlockSpec(memory_space=pl.ANY)
    hbm = pl.BlockSpec(memory_space=pltpu.HBM)
    in_specs = [pl.BlockSpec(memory_space=pltpu.SMEM)] * len(scalars) + [whole] * len(operands)
    return pl.pallas_call(
        kernel,
        out_shape=[jax.ShapeDtypeStruct(s, d) for s, d in list(shapes) + [FLAG] * flag],
        in_specs=in_specs + [hbm] * len(far) + [anywhere] * len(tokens),
        out_specs=[hbm if direct else whole] * len(shapes) + [whole] * flag,
        scratch_shapes=list(scratch),
        compiler_params=pltpu.CompilerParams(vmem_limit_bytes=VMEM_LIMIT),
        cost_estimate=pl.CostEstimate(
            flops=int(micros * 1000000000), bytes_accessed=0, transcendentals=0
        ),
    )(*[v[None] for v in scalars], *operands, *far, *tokens)


def after(value, *tokens):
    anywhere = pl.BlockSpec(memory_space=pl.ANY)
    return pl.pallas_call(
        lambda *refs: None,
        out_shape=jax.ShapeDtypeStruct(value.shape, value.dtype),
        in_specs=[anywhere] * (1 + len(tokens)),
        out_specs=anywhere,
        input_output_aliases={0: 0},
        compiler_params=pltpu.CompilerParams(vmem_limit_bytes=TIE_LIMIT),
        cost_estimate=pl.CostEstimate(flops=0, bytes_accessed=0, transcendentals=0),
    )(value, *tokens)


def fetch(sources, targets, sems):
    copies = [
        pltpu.make_async_copy(source, target, sems.at[i])
        for i, (source, target) in enumerate(zip(sources, targets))
    ]
    for copy in copies:
        copy.start()
    return copies


def middle(pre_gate, pre_up, hidden_grad):
    sigmoid_gate = jax.nn.sigmoid(pre_gate)
    active = pre_gate * sigmoid_gate
    hidden = (active * pre_up).astype(jnp.bfloat16)
    gate_delta = (
        hidden_grad * pre_up * sigmoid_gate * (1.0 + pre_gate * (1.0 - sigmoid_gate))
    ).astype(jnp.bfloat16)
    up_delta = (hidden_grad * active).astype(jnp.bfloat16)
    return hidden, jnp.concatenate([gate_delta, up_delta], axis=1)


def columns(place, part, k, start, size):
    return pl.ds(pl.multiple_of((place ^ k) * part + start, 128), size)


def write_terms(place, part, units, hidden, delta, normed, cot, send, keep):
    half = part // 2
    for k in (1, 3, 0, 2):
        for side in range(2):
            at = columns(place, part, k, side * half, half)
            if k % 2:
                out = send[k // 2 * 2 + side]
                into = slice(0, half)
            else:
                out = keep
                into = slice(k // 2 * part + side * half, k // 2 * part + (side + 1) * half)
            out[:2 * units, into] = mul(delta, normed[:, at], TN).astype(out.dtype)
            out[2 * units:, into] = mul(hidden, cot[:, at], TN).astype(out.dtype)


def pack_kernel(part, units, place_ref, place_1, place_2, gate, up, down, low, high, other, gates, ups, downs, sems):
    place = place_ref[0]
    half = part // 2
    sources, targets = [], []
    for i, k in enumerate((0, 2)):
        at = columns(place, part, k, 0, part)
        sources += [gate.at[at, :], up.at[at, :], down.at[:, at]]
        targets += [gates.at[i], ups.at[i], downs.at[i]]
    copies = fetch(sources, targets, sems)
    for copy in copies[:3]:
        copy.wait()
    for out, start in ((low, 0), (high, half)):
        out[:, :units] = gates[0, start:start + half, :]
        out[:, units:2 * units] = ups[0, start:start + half, :]
        out[:, 2 * units:] = jnp.transpose(downs[0, :, start:start + half])
    for copy in copies[3:]:
        copy.wait()
    other[:, :units] = gates[1]
    other[:, units:2 * units] = ups[1]
    other[:, 2 * units:] = jnp.transpose(downs[1])


def own_kernel(gain, tokens_far, cot_far, gate_far, up_far, down_far, *rest):
    cot, normed, inverse_ref, hidden_ref, delta_ref, tokens, gate, up, down, sems = rest[-10:]
    copies = fetch(
        (tokens_far, cot_far, gate_far, up_far, down_far), (tokens, cot, gate, up, down), sems
    )
    copies[0].wait()

    def strip(i, carry):
        rows = pl.ds(pl.multiple_of(i * STRIP, STRIP), STRIP)
        wide = tokens[rows, :].astype(jnp.float32)
        inverse = lax.rsqrt(jnp.mean(wide * wide, axis=-1, keepdims=True) + epsilon)
        inverse_ref[rows, :] = inverse
        normed[rows, :] = (wide * inverse * gain[...]).astype(jnp.bfloat16)
        return carry

    lax.fori_loop(0, tokens.shape[0] // STRIP, strip, 0)
    for copy in copies[1:]:
        copy.wait()
    hidden, delta = middle(
        mul(normed[...], gate[...]), mul(normed[...], up[...]), mul(cot[...], down[...], NT)
    )
    hidden_ref[...] = hidden
    delta_ref[...] = delta


def terms_kernel(part, units, place_ref, normed, cot, hidden, delta, *rest):
    write_terms(
        place_ref[0], part, units, hidden[...], delta[...], normed, cot, rest[-5:-1], rest[-1]
    )


def shard_kernel(part, units, layout, place_ref, normed, cot, *rest):
    pieces = rest[:len(layout)]
    hidden_ref, delta_ref = rest[-7:-5]
    send, keep = rest[-5:-1], rest[-1]
    place = place_ref[0]
    pre = None
    grad = None
    for (k, start, size), piece in zip(layout, pieces):
        at = columns(place, part, k, start, size)
        pre_here = mul(normed[:, at], piece[:, :2 * units])
        grad_here = mul(cot[:, at], piece[:, 2 * units:])
        pre = pre_here if pre is None else pre + pre_here
        grad = grad_here if grad is None else grad + grad_here
    hidden, delta = middle(pre[:, :units], pre[:, units:], grad)
    hidden_ref[...] = hidden
    delta_ref[...] = delta
    write_terms(place, part, units, hidden, delta, normed, cot, send, keep)


def summed(part, keep, arrived):
    half = part // 2
    return [keep[:, i * half:(i + 1) * half] + arrived[i][...].astype(jnp.float32) for i in range(DP)]


def add_kernel(part, keep, *rest):
    half = part // 2
    total = summed(part, keep, rest[:DP])
    out, mine = rest[-2:]
    mine[:, :half] = total[0]
    mine[:, half:] = total[1]
    out[:, :half] = total[2].astype(jnp.bfloat16)
    out[:, half:] = total[3].astype(jnp.bfloat16)


def last_add_kernel(part, keep, mine_1, here_1, *rest):
    half = part // 2
    total = summed(part, keep, rest[:DP])
    low, high, mine, near = rest[-4:]
    mine[:, :half] = total[0]
    mine[:, half:] = total[1]
    low[...] = total[2].astype(jnp.bfloat16)
    high[...] = total[3].astype(jnp.bfloat16)
    near[...] = (mine_1[...] + here_1[...].astype(jnp.float32)).astype(jnp.bfloat16)


def hop_kernel(start, mine, arrived, *rest):
    size = arrived.shape[1]
    total = mine[:, start:start + size] + arrived[...].astype(jnp.float32)
    if start == 0:
        later, out, later_out = rest[0], rest[-2], rest[-1]
        later_out[...] = later[...]
    else:
        out = rest[-1]
    out[...] = total.astype(jnp.bfloat16)


def final_kernel(units, mine, here, near, low, high, gate, up, down, keep_g, keep_u, keep_d, sems):
    half = low.shape[1]
    for start, last in ((0, low), (half, high)):
        at = slice(start, start + half)
        total = mine[:, at] + here[:, at].astype(jnp.float32) + near[:, at].astype(jnp.float32)
        total = (total + last[...].astype(jnp.float32)) * grad_scale
        keep_g[at, :] = jnp.transpose(total[:units])
        keep_u[at, :] = jnp.transpose(total[units:2 * units])
        keep_d[:, at] = total[2 * units:]
    for copy in fetch((keep_g, keep_u, keep_d), (gate, up, down), sems):
        copy.wait()


def strips(rows, kept, far, sems, body):
    group = rows // DP
    copies = []
    for g in range(DP):
        def strip(i, carry):
            body(pl.ds(pl.multiple_of(g * group + i * STRIP, STRIP), STRIP))
            return carry

        lax.fori_loop(0, group // STRIP, strip, 0)
        here = pl.ds(g * group, group)
        copies.append(pltpu.make_async_copy(kept.at[here, :], far.at[here, :], sems.at[g]))
        copies[-1].start()
    for copy in copies:
        copy.wait()


def forward_out_kernel(part, units, layouts, place_1, place_2, hidden_0, hidden_1, hidden_2, *rest):
    count = len(layouts[0]) + len(layouts[1])
    pieces, rest = rest[:count], rest[count:]
    tokens_far, down_far = rest[:2]
    block_out, flag, tokens, down, mlp, kept, in_sems, out_sems = rest[-8:]
    flag[...] = jnp.zeros_like(flag)
    copies = fetch((down_far, tokens_far), (down, tokens), in_sems)
    copies[0].wait()
    for j in range(DP):
        at = pl.ds(j * part, part)
        mlp[:, at] = mul(hidden_0[...], down[:, at])
    used = 0
    for place_ref, layout, hidden in ((place_1, layouts[0], hidden_1), (place_2, layouts[1], hidden_2)):
        place = place_ref[0]
        for k, start, size in layout:
            at = columns(place, part, k, start, size)
            mlp[:, at] += mul(hidden[...], pieces[used][:, 2 * units:], NT)
            used += 1
    copies[1].wait()

    def body(rows):
        kept[rows, :] = (tokens[rows, :].astype(jnp.float32) + mlp[rows, :]).astype(jnp.bfloat16)

    strips(tokens.shape[0], kept, block_out, out_sems, body)


def backward_out_kernel(part, units, layouts, place_1, place_2, cot, gain, inverse_ref, delta_0, delta_1, delta_2, *rest):
    count = len(layouts[0]) + len(layouts[1])
    pieces, rest = rest[:count], rest[count:]
    tokens_far, gate_far, up_far, input_grad, flag, tokens, gate, up, dnormed, kept, in_sems, out_sems = rest
    flag[...] = jnp.zeros_like(flag)
    copies = fetch((gate_far, up_far, tokens_far), (gate, up, tokens), in_sems)
    for copy in copies[:2]:
        copy.wait()
    for j in range(DP):
        at = pl.ds(j * part, part)
        dnormed[:, at] = mul(delta_0[:, :units], gate[at, :], NT) + mul(
            delta_0[:, units:], up[at, :], NT
        )
    used = 0
    for place_ref, layout, delta in ((place_1, layouts[0], delta_1), (place_2, layouts[1], delta_2)):
        place = place_ref[0]
        for k, start, size in layout:
            at = columns(place, part, k, start, size)
            dnormed[:, at] += mul(delta[...], pieces[used][:, :2 * units], NT)
            used += 1
    copies[2].wait()

    def body(rows):
        wide = tokens[rows, :].astype(jnp.float32)
        inverse = inverse_ref[rows, :]
        scaled = wide * inverse
        along = dnormed[rows, :] * gain[...]
        norm_back = inverse * (along - scaled * jnp.mean(along * scaled, axis=-1, keepdims=True))
        kept[rows, :] = (cot[rows, :].astype(jnp.float32) + norm_back).astype(jnp.bfloat16)

    strips(tokens.shape[0], kept, input_grad, out_sems, body)


def shards(tokens, cotangent, norm_gain, gate_weight, up_weight, down_weight):
    place = lax.axis_index("dp")
    block = lax.axis_index("blk")
    span = half_of(lax.axis_size("blk"))
    rows, model = tokens.shape
    part = model // DP
    half = part // 2
    units = gate_weight.shape[1]
    width = 3 * units
    bf16, f32 = jnp.bfloat16, jnp.float32
    place_1 = place ^ jnp.where(block % span < 1, 2, 0)
    place_2 = place ^ jnp.where(block % span < 2, 2, 0)
    gate_weight, up_weight, down_weight, tokens = (
        pltpu.with_memory_space_constraint(v, pltpu.HBM)
        for v in (gate_weight, up_weight, down_weight, tokens)
    )
    weights = [gate_weight, up_weight, down_weight]
    gain = norm_gain[None, :]
    dma = pltpu.SemaphoreType.DMA

    low, high, other = call(
        functools.partial(pack_kernel, part, units), [],
        [((half, width), bf16)] * 2 + [((part, width), bf16)], 2, far=weights,
        scalars=(place, place_1, place_2),
        scratch=[pltpu.VMEM((2, part, units), bf16)] * 2
        + [pltpu.VMEM((2, units, part), bf16), dma((6,))],
    )
    one_a = forward(low)
    one_b = forward(high)
    two_z = around_first(other)

    acts = [((rows, units), bf16), ((rows, 2 * units), bf16)]
    terms = [((width, half), bf16)] * 4 + [((width, 2 * part), f32)]

    cot, normed, inverse, hidden_0, delta_0 = call(
        own_kernel, [gain], [((rows, model), bf16)] * 2 + [((rows, 1), f32)] + acts, 4,
        far=[tokens, cotangent] + weights, tokens=(other,),
        scratch=[pltpu.VMEM((rows, model), bf16)] + [pltpu.VMEM((model, units), bf16)] * 2
        + [pltpu.VMEM((units, model), bf16), dma((5,))],
    )

    one_a = after(one_a, hidden_0)
    *send, keep = call(
        functools.partial(terms_kernel, part, units), [normed, cot, hidden_0, delta_0], terms, 3,
        scalars=(place,), tokens=(one_a,),
    )
    one_xa = swap(one_a, 2)
    two_a = forward(one_a)
    one_b = after(one_b, keep, one_xa)
    one_xb = swap(one_b, 2)
    two_b = forward(one_b)
    two_z = around_second(two_z)
    ones = [one_a, one_b, one_xa, one_xb]
    ones = ones + [swap(v, 1) for v in ones]
    layout_1 = [(k, start, half) for k in (0, 2, 1, 3) for start in (0, half)]
    twos = [two_a, two_b, two_z]
    twos = twos + [swap(v, 1) for v in twos]
    layout_2 = [(0, 0, half), (0, half, half), (2, 0, part), (1, 0, half), (1, half, half), (3, 0, part)]

    def add(keep, send, tokens=()):
        return call(
            functools.partial(add_kernel, part), [keep] + [swap(v, 1) for v in send],
            [((width, part), bf16), ((width, part), f32)], 1, tokens=tokens,
        )

    out_0, mine_0 = add(keep, send, (one_xb, two_a))
    here_0 = swap(out_0, 2)

    hidden_1, delta_1, *send, keep = call(
        functools.partial(shard_kernel, part, units, layout_1), [normed, cot] + ones,
        acts + terms, 4, scalars=(place_1,), tokens=(out_0, two_b),
    )
    out_1, mine_1 = add(keep, send, (here_0,))
    here_1 = swap(out_1, 2)

    hidden_2, delta_2, *send, keep = call(
        functools.partial(shard_kernel, part, units, layout_2), [normed, cot] + twos,
        acts + terms, 4, scalars=(place_2,), tokens=(hidden_1,),
    )
    input_grad, flag_backward = call(
        functools.partial(backward_out_kernel, part, units, (layout_1, layout_2)),
        [cot, gain, inverse, delta_0, delta_1, delta_2] + ones + twos,
        [((rows, model), bf16)], 5,
        far=[tokens, gate_weight, up_weight], scalars=(place_1, place_2), direct=True, flag=True,
        scratch=[
            pltpu.VMEM((rows, model), bf16), pltpu.VMEM((model, units), bf16),
            pltpu.VMEM((model, units), bf16), pltpu.VMEM((rows, model), f32),
            pltpu.VMEM((rows, model), bf16), dma((3,)), dma((DP,)),
        ],
    )

    low_2, high_2, mine_2, near = call(
        functools.partial(last_add_kernel, part),
        [keep, mine_1, here_1] + [swap(v, 1) for v in send],
        [((width, half), bf16)] * 2 + [((width, part), f32), ((width, part), bf16)], 1,
        tokens=(flag_backward,),
    )
    near = backward(near)

    block_out, flag_forward = call(
        functools.partial(forward_out_kernel, part, units, (layout_1, layout_2)),
        [hidden_0, hidden_1, hidden_2] + ones + twos, [((rows, model), bf16)], 4,
        far=[tokens, down_weight], tokens=(low_2,), scalars=(place_1, place_2), direct=True, flag=True,
        scratch=[
            pltpu.VMEM((rows, model), bf16), pltpu.VMEM((units, model), bf16),
            pltpu.VMEM((rows, model), f32), pltpu.VMEM((rows, model), bf16), dma((2,)), dma((DP,)),
        ],
    )
    sum_low, high_2 = call(
        functools.partial(hop_kernel, 0), [mine_2, swap(low_2, 2), high_2],
        [((width, half), bf16)] * 2, 0.5, tokens=(flag_forward,),
    )
    sum_low = back_two(sum_low)
    sum_high, = call(
        functools.partial(hop_kernel, half), [mine_2, swap(high_2, 2)],
        [((width, half), bf16)], 0.5, tokens=(near,),
    )
    sum_high = back_two(sum_high)

    gate_grad, up_grad, down_grad = call(
        functools.partial(final_kernel, units), [mine_0, here_0, near, sum_low, sum_high],
        [((part, units), f32)] * 2 + [((units, part), f32)], 2, direct=True,
        scratch=[pltpu.VMEM((part, units), f32)] * 2 + [pltpu.VMEM((units, part), f32), dma((3,))],
    )
    return block_out, input_grad, gate_grad, up_grad, down_grad


def solution(mesh):
    in_specs = (
        P(("dp", "blk"), None),
        P(("dp", "blk"), None),
        P(),
        P(None, "blk"),
        P(None, "blk"),
        P("blk", None),
    )
    out_specs = (
        P(("dp", "blk"), None),
        P(("dp", "blk"), None),
        P("dp", "blk"),
        P("dp", "blk"),
        P("blk", "dp"),
    )
    return jax.shard_map(shards, mesh=mesh, in_specs=in_specs, out_specs=out_specs, check_vma=False)
```

```python
import functools

import jax
import jax.numpy as jnp
from jax import lax
from jax.experimental import pallas as pl
from jax.experimental.pallas import tpu as pltpu
from jax.sharding import PartitionSpec as P

DP = 4
PIECES = 3
RING = 4
TIE_LIMIT = 1024 * 1024
VMEM_LIMIT = 12 * 1024 * 1024


epsilon = 1e-05
grad_scale = 0.0625

BOTH = ("dp", "blk")
NN = (((1,), (0,)), ((), ()))
FLAG = ((8, 128), jnp.float32)
NT = (((1,), (1,)), ((), ()))
TN = (((0,), (0,)), ((), ()))
STRIP = 16


def mul(left, right, dims=NN):
    return lax.dot_general(left, right, dims, preferred_element_type=jnp.float32)


def move(value, target):
    count = lax.axis_size("blk")
    pairs = []
    for place in range(DP):
        for block in range(count):
            to_place, to_block = target(place, block)
            pairs.append((place * count + block, to_place * count + to_block % count))
    return lax.ppermute(value, BOTH, pairs)


def swap(value, bit):
    return lax.ppermute(value, "dp", [(source, source ^ bit) for source in range(DP)])


def turn(block, step):
    return block // RING * RING + (block + step) % RING


def half_of(count):
    return count // 2


def forward(value):
    def target(place, block):
        half = half_of(lax.axis_size("blk"))
        return place ^ (2 if block % half == half - 1 else 0), block + 1

    return move(value, target)


def backward(value):
    def target(place, block):
        half = half_of(lax.axis_size("blk"))
        return place ^ (2 if block % half == 0 else 0), block - 1

    return move(value, target)


def back_two(value):
    def target(place, block):
        half = half_of(lax.axis_size("blk"))
        return place ^ (2 if block % half < 2 else 0), block - 2

    return move(value, target)


def around_first(value):
    return move(value, lambda place, block: (place, turn(block, -1)))


def around_second(value):
    def target(place, block):
        half = half_of(lax.axis_size("blk"))
        source = turn(block, 1)
        return place ^ (2 if source % half >= half - 2 else 0), source + 2

    return move(value, target)


def call(kernel, operands, shapes, micros, far=(), tokens=(), scalars=(), scratch=(), direct=False, flag=False):
    whole = pl.BlockSpec(memory_space=pltpu.VMEM)
    anywhere = pl.BlockSpec(memory_space=pl.ANY)
    hbm = pl.BlockSpec(memory_space=pltpu.HBM)
    in_specs = [pl.BlockSpec(memory_space=pltpu.SMEM)] * len(scalars) + [whole] * len(operands)
    return pl.pallas_call(
        kernel,
        out_shape=[jax.ShapeDtypeStruct(s, d) for s, d in list(shapes) + [FLAG] * flag],
        in_specs=in_specs + [hbm] * len(far) + [anywhere] * len(tokens),
        out_specs=[hbm if direct else whole] * len(shapes) + [whole] * flag,
        scratch_shapes=list(scratch),
        compiler_params=pltpu.CompilerParams(vmem_limit_bytes=VMEM_LIMIT),
        cost_estimate=pl.CostEstimate(
            flops=int(micros * 1000000000), bytes_accessed=0, transcendentals=0
        ),
    )(*[v[None] for v in scalars], *operands, *far, *tokens)


def after(value, *tokens, micros=0):
    anywhere = pl.BlockSpec(memory_space=pl.ANY)
    return pl.pallas_call(
        lambda *refs: None,
        out_shape=jax.ShapeDtypeStruct(value.shape, value.dtype),
        in_specs=[anywhere] * (1 + len(tokens)),
        out_specs=anywhere,
        input_output_aliases={0: 0},
        compiler_params=pltpu.CompilerParams(vmem_limit_bytes=TIE_LIMIT),
        cost_estimate=pl.CostEstimate(
            flops=int(micros * 10**9), bytes_accessed=0, transcendentals=0
        ),
    )(value, *tokens)


def fetch(sources, targets, sems):
    copies = [
        pltpu.make_async_copy(source, target, sems.at[i])
        for i, (source, target) in enumerate(zip(sources, targets))
    ]
    for copy in copies:
        copy.start()
    return copies


def middle(pre_gate, pre_up, hidden_grad):
    sigmoid_gate = jax.nn.sigmoid(pre_gate)
    active = pre_gate * sigmoid_gate
    hidden = (active * pre_up).astype(jnp.bfloat16)
    gate_delta = (
        hidden_grad * pre_up * sigmoid_gate * (1.0 + pre_gate * (1.0 - sigmoid_gate))
    ).astype(jnp.bfloat16)
    up_delta = (hidden_grad * active).astype(jnp.bfloat16)
    return hidden, jnp.concatenate([gate_delta, up_delta], axis=1)


def columns(place, part, k, start, size):
    return pl.ds(pl.multiple_of((place ^ k) * part + start, 128), size)


def write_terms(place, part, units, hidden, delta, normed, cot, send, keep):
    size = part // PIECES
    for k in (1, 3, 0, 2):
        for side in range(PIECES):
            at = columns(place, part, k, side * size, size)
            start = k // 2 * part + side * size
            out = keep
            if k % 2:
                out = send[start // (2 * size)]
                start = start % (2 * size)
            into = slice(start, start + size)
            out[:2 * units, into] = mul(delta, normed[:, at], TN).astype(out.dtype)
            out[2 * units:, into] = mul(hidden, cot[:, at], TN).astype(out.dtype)


def pack_kernel(part, units, place_ref, place_1, place_2, gate, up, down, *rest):
    outs, (gates, ups, downs, sems) = rest[:2], rest[2:]
    place = place_ref[0]
    sources, targets = [], []
    for i, k in enumerate((0, 2)):
        at = columns(place, part, k, 0, part)
        sources += [gate.at[at, :], up.at[at, :], down.at[:, at]]
        targets += [gates.at[i], ups.at[i], downs.at[i]]
    copies = fetch(sources, targets, sems)
    for i, out in enumerate(outs):
        for copy in copies[3 * i:3 * i + 3]:
            copy.wait()
        out[:, :units] = gates[i]
        out[:, units:2 * units] = ups[i]
        out[:, 2 * units:] = jnp.transpose(downs[i])


def own_kernel(gain, tokens_far, cot_far, gate_far, up_far, down_far, *rest):
    cot, normed, inverse_ref, hidden_ref, delta_ref, tokens, gate, up, down, sems = rest[-10:]
    copies = fetch(
        (tokens_far, cot_far, gate_far, up_far, down_far), (tokens, cot, gate, up, down), sems
    )
    copies[0].wait()

    def strip(i, carry):
        rows = pl.ds(pl.multiple_of(i * STRIP, STRIP), STRIP)
        wide = tokens[rows, :].astype(jnp.float32)
        inverse = lax.rsqrt(jnp.mean(wide * wide, axis=-1, keepdims=True) + epsilon)
        inverse_ref[rows, :] = inverse
        normed[rows, :] = (wide * inverse * gain[...]).astype(jnp.bfloat16)
        return carry

    lax.fori_loop(0, tokens.shape[0] // STRIP, strip, 0)
    for copy in copies[1:]:
        copy.wait()
    hidden, delta = middle(
        mul(normed[...], gate[...]), mul(normed[...], up[...]), mul(cot[...], down[...], NT)
    )
    hidden_ref[...] = hidden
    delta_ref[...] = delta


def terms_kernel(part, units, place_ref, normed, cot, hidden, delta, *rest):
    write_terms(
        place_ref[0], part, units, hidden[...], delta[...], normed, cot, rest[-PIECES - 1:-1], rest[-1]
    )


def shard_kernel(part, units, layout, place_ref, normed, cot, *rest):
    pieces = rest[:len(layout)]
    hidden_ref, delta_ref = rest[-PIECES - 3:-PIECES - 1]
    send, keep = rest[-PIECES - 1:-1], rest[-1]
    place = place_ref[0]
    pre = None
    grad = None
    for (k, start, size), piece in zip(layout, pieces):
        at = columns(place, part, k, start, size)
        pre_here = mul(normed[:, at], piece[:, :2 * units])
        grad_here = mul(cot[:, at], piece[:, 2 * units:])
        pre = pre_here if pre is None else pre + pre_here
        grad = grad_here if grad is None else grad + grad_here
    hidden, delta = middle(pre[:, :units], pre[:, units:], grad)
    hidden_ref[...] = hidden
    delta_ref[...] = delta
    write_terms(place, part, units, hidden, delta, normed, cot, send, keep)


def summed(part, keep, arrived):
    size = 2 * part // PIECES
    total = [
        keep[:, i * size:(i + 1) * size] + arrived[i][...].astype(jnp.float32)
        for i in range(PIECES)
    ]
    return jnp.concatenate(total, axis=1)


def add_kernel(part, keep, *rest):
    total = summed(part, keep, rest[:PIECES])
    out, mine = rest[-2:]
    mine[...] = total[:, :part]
    out[...] = total[:, part:].astype(jnp.bfloat16)


def last_add_kernel(part, keep, mine_1, here_1, *rest):
    half = part // 2
    total = summed(part, keep, rest[:PIECES])
    low, high, mine, near = rest[-4:]
    mine[...] = total[:, :part]
    low[...] = total[:, part:part + half].astype(jnp.bfloat16)
    high[...] = total[:, part + half:].astype(jnp.bfloat16)
    near[...] = (mine_1[...] + here_1[...].astype(jnp.float32)).astype(jnp.bfloat16)


def hop_kernel(start, mine, arrived, *rest):
    size = arrived.shape[1]
    total = mine[:, start:start + size] + arrived[...].astype(jnp.float32)
    if start == 0:
        later, out, later_out = rest[0], rest[-2], rest[-1]
        later_out[...] = later[...]
    else:
        out = rest[-1]
    out[...] = total.astype(jnp.bfloat16)


def final_kernel(units, mine, here, near, low, high, gate, up, down, keep_g, keep_u, keep_d, sems):
    half = low.shape[1]
    for start, last in ((0, low), (half, high)):
        at = slice(start, start + half)
        total = mine[:, at] + here[:, at].astype(jnp.float32) + near[:, at].astype(jnp.float32)
        total = (total + last[...].astype(jnp.float32)) * grad_scale
        keep_g[at, :] = jnp.transpose(total[:units])
        keep_u[at, :] = jnp.transpose(total[units:2 * units])
        keep_d[:, at] = total[2 * units:]
    for copy in fetch((keep_g, keep_u, keep_d), (gate, up, down), sems):
        copy.wait()


def strips(rows, kept, far, sems, body):
    group = rows // DP
    copies = []
    for g in range(DP):
        def strip(i, carry):
            body(pl.ds(pl.multiple_of(g * group + i * STRIP, STRIP), STRIP))
            return carry

        lax.fori_loop(0, group // STRIP, strip, 0)
        here = pl.ds(g * group, group)
        copies.append(pltpu.make_async_copy(kept.at[here, :], far.at[here, :], sems.at[g]))
        copies[-1].start()
    for copy in copies:
        copy.wait()


def forward_out_kernel(part, units, layouts, place_1, place_2, hidden_0, hidden_1, hidden_2, *rest):
    count = len(layouts[0]) + len(layouts[1])
    pieces, rest = rest[:count], rest[count:]
    tokens_far, down_far = rest[:2]
    block_out, flag, tokens, down, mlp, kept, in_sems, out_sems = rest[-8:]
    flag[...] = jnp.zeros_like(flag)
    copies = fetch((down_far, tokens_far), (down, tokens), in_sems)
    copies[0].wait()
    for j in range(DP):
        at = pl.ds(j * part, part)
        mlp[:, at] = mul(hidden_0[...], down[:, at])
    used = 0
    for place_ref, layout, hidden in ((place_1, layouts[0], hidden_1), (place_2, layouts[1], hidden_2)):
        place = place_ref[0]
        for k, start, size in layout:
            at = columns(place, part, k, start, size)
            mlp[:, at] += mul(hidden[...], pieces[used][:, 2 * units:], NT)
            used += 1
    copies[1].wait()

    def body(rows):
        kept[rows, :] = (tokens[rows, :].astype(jnp.float32) + mlp[rows, :]).astype(jnp.bfloat16)

    strips(tokens.shape[0], kept, block_out, out_sems, body)


def backward_out_kernel(part, units, layouts, place_1, place_2, cot, gain, inverse_ref, delta_0, delta_1, delta_2, *rest):
    count = len(layouts[0]) + len(layouts[1])
    pieces, rest = rest[:count], rest[count:]
    tokens_far, gate_far, up_far, input_grad, flag, tokens, gate, up, dnormed, kept, in_sems, out_sems = rest
    flag[...] = jnp.zeros_like(flag)
    copies = fetch((gate_far, up_far, tokens_far), (gate, up, tokens), in_sems)
    for copy in copies[:2]:
        copy.wait()
    for j in range(DP):
        at = pl.ds(j * part, part)
        dnormed[:, at] = mul(delta_0[:, :units], gate[at, :], NT) + mul(
            delta_0[:, units:], up[at, :], NT
        )
    used = 0
    for place_ref, layout, delta in ((place_1, layouts[0], delta_1), (place_2, layouts[1], delta_2)):
        place = place_ref[0]
        for k, start, size in layout:
            at = columns(place, part, k, start, size)
            dnormed[:, at] += mul(delta[...], pieces[used][:, :2 * units], NT)
            used += 1
    copies[2].wait()

    def body(rows):
        wide = tokens[rows, :].astype(jnp.float32)
        inverse = inverse_ref[rows, :]
        scaled = wide * inverse
        along = dnormed[rows, :] * gain[...]
        norm_back = inverse * (along - scaled * jnp.mean(along * scaled, axis=-1, keepdims=True))
        kept[rows, :] = (cot[rows, :].astype(jnp.float32) + norm_back).astype(jnp.bfloat16)

    strips(tokens.shape[0], kept, input_grad, out_sems, body)


def shards(tokens, cotangent, norm_gain, gate_weight, up_weight, down_weight):
    place = lax.axis_index("dp")
    block = lax.axis_index("blk")
    span = half_of(lax.axis_size("blk"))
    rows, model = tokens.shape
    part = model // DP
    half = part // 2
    units = gate_weight.shape[1]
    width = 3 * units
    bf16, f32 = jnp.bfloat16, jnp.float32
    place_1 = place ^ jnp.where(block % span < 1, 2, 0)
    place_2 = place ^ jnp.where(block % span < 2, 2, 0)
    gate_weight, up_weight, down_weight, tokens = (
        pltpu.with_memory_space_constraint(v, pltpu.HBM)
        for v in (gate_weight, up_weight, down_weight, tokens)
    )
    weights = [gate_weight, up_weight, down_weight]
    gain = norm_gain[None, :]
    dma = pltpu.SemaphoreType.DMA

    piece, other = call(
        functools.partial(pack_kernel, part, units), [], [((part, width), bf16)] * 2, 2,
        far=weights, scalars=(place, place_1, place_2),
        scratch=[pltpu.VMEM((2, part, units), bf16)] * 2
        + [pltpu.VMEM((2, units, part), bf16), dma((6,))],
    )
    one = forward(piece)
    two_z = around_first(other)

    acts = [((rows, units), bf16), ((rows, 2 * units), bf16)]
    terms = [((width, 2 * part // PIECES), bf16)] * PIECES + [((width, 2 * part), f32)]

    cot, normed, inverse, hidden_0, delta_0 = call(
        own_kernel, [gain], [((rows, model), bf16)] * 2 + [((rows, 1), f32)] + acts, 5,
        far=[tokens, cotangent] + weights, tokens=(other,),
        scratch=[pltpu.VMEM((rows, model), bf16)] + [pltpu.VMEM((model, units), bf16)] * 2
        + [pltpu.VMEM((units, model), bf16), dma((5,))],
    )

    *send, keep = call(
        functools.partial(terms_kernel, part, units), [normed, cot, hidden_0, delta_0], terms, 5,
        scalars=(place,),
    )
    def add(keep, send, tokens=()):
        return call(
            functools.partial(add_kernel, part), [keep] + [swap(v, 1) for v in send],
            [((width, part), bf16), ((width, part), f32)], 1, tokens=tokens,
        )

    out_0, mine_0 = add(keep, send)
    here_0 = swap(out_0, 2)
    one = after(one, out_0, two_z)
    one_x = swap(one, 2)
    two = forward(one)
    two_z = around_second(two_z)
    ones = [one, one_x, swap(one, 1), swap(one_x, 1)]
    twos = [two, two_z, swap(two, 1), swap(two_z, 1)]
    layout = [(k, 0, part) for k in (0, 2, 1, 3)]

    hidden_1, delta_1, *send, keep = call(
        functools.partial(shard_kernel, part, units, layout), [normed, cot] + ones,
        acts + terms, 4, scalars=(place_1,), tokens=(out_0, two, two_z),
    )
    keep_1, send_1 = keep, send

    hidden_2, delta_2, *send, keep = call(
        functools.partial(shard_kernel, part, units, layout), [normed, cot] + twos,
        acts + terms, 4, scalars=(place_2,), tokens=(hidden_1,),
    )
    input_grad, flag_backward = call(
        functools.partial(backward_out_kernel, part, units, (layout, layout)),
        [cot, gain, inverse, delta_0, delta_1, delta_2] + ones + twos,
        [((rows, model), bf16)], 5,
        far=[tokens, gate_weight, up_weight], scalars=(place_1, place_2), direct=True, flag=True,
        scratch=[
            pltpu.VMEM((rows, model), bf16), pltpu.VMEM((model, units), bf16),
            pltpu.VMEM((model, units), bf16), pltpu.VMEM((rows, model), f32),
            pltpu.VMEM((rows, model), bf16), dma((3,)), dma((DP,)),
        ],
    )

    here_0 = after(here_0, hidden_1, micros=14)
    out_1, mine_1 = add(keep_1, send_1, (here_0,))
    here_1 = swap(out_1, 2)
    low_2, high_2, mine_2, near = call(
        functools.partial(last_add_kernel, part),
        [keep, mine_1, here_1] + [swap(v, 1) for v in send],
        [((width, half), bf16)] * 2 + [((width, part), f32), ((width, part), bf16)], 1,
        tokens=(flag_backward,),
    )
    near = after(backward(near), micros=8)

    block_out, flag_forward = call(
        functools.partial(forward_out_kernel, part, units, (layout, layout)),
        [hidden_0, hidden_1, hidden_2] + ones + twos, [((rows, model), bf16)], 4,
        far=[tokens, down_weight], tokens=(low_2,), scalars=(place_1, place_2), direct=True, flag=True,
        scratch=[
            pltpu.VMEM((rows, model), bf16), pltpu.VMEM((units, model), bf16),
            pltpu.VMEM((rows, model), f32), pltpu.VMEM((rows, model), bf16), dma((2,)), dma((DP,)),
        ],
    )
    sum_low, high_2 = call(
        functools.partial(hop_kernel, 0), [mine_2, swap(low_2, 2), high_2],
        [((width, half), bf16)] * 2, 0.5, tokens=(flag_forward,),
    )
    sum_low = back_two(sum_low)
    sum_high, = call(
        functools.partial(hop_kernel, half), [mine_2, swap(high_2, 2)],
        [((width, half), bf16)], 0.5,
    )
    sum_high = back_two(sum_high)

    gate_grad, up_grad, down_grad = call(
        functools.partial(final_kernel, units), [mine_0, here_0, near, sum_low, sum_high],
        [((part, units), f32)] * 2 + [((units, part), f32)], 2, direct=True,
        scratch=[pltpu.VMEM((part, units), f32)] * 2 + [pltpu.VMEM((units, part), f32), dma((3,))],
    )
    return block_out, input_grad, gate_grad, up_grad, down_grad


def solution(mesh):
    in_specs = (
        P(("dp", "blk"), None),
        P(("dp", "blk"), None),
        P(),
        P(None, "blk"),
        P(None, "blk"),
        P("blk", None),
    )
    out_specs = (
        P(("dp", "blk"), None),
        P(("dp", "blk"), None),
        P("dp", "blk"),
        P("dp", "blk"),
        P("blk", "dp"),
    )
    return jax.shard_map(shards, mesh=mesh, in_specs=in_specs, out_specs=out_specs, check_vma=False)
```

```python
import functools

import jax
import jax.numpy as jnp
from jax import lax
from jax.experimental import pallas as pl
from jax.experimental.pallas import tpu as pltpu
from jax.sharding import PartitionSpec as P

DP = 4
PIECES = 3
RING = 4
TIE_LIMIT = 1024 * 1024
VMEM_LIMIT = 12 * 1024 * 1024


epsilon = 1e-05
grad_scale = 0.0625

BOTH = ("dp", "blk")
NN = (((1,), (0,)), ((), ()))
FLAG = ((8, 128), jnp.float32)
NT = (((1,), (1,)), ((), ()))
TN = (((0,), (0,)), ((), ()))
STRIP = 16


def mul(left, right, dims=NN):
    return lax.dot_general(left, right, dims, preferred_element_type=jnp.float32)


def move(value, target):
    count = lax.axis_size("blk")
    pairs = []
    for place in range(DP):
        for block in range(count):
            to_place, to_block = target(place, block)
            pairs.append((place * count + block, to_place * count + to_block % count))
    return lax.ppermute(value, BOTH, pairs)


def swap(value, bit):
    return lax.ppermute(value, "dp", [(source, source ^ bit) for source in range(DP)])


def turn(block, step):
    return block // RING * RING + (block + step) % RING


def half_of(count):
    return count // 2


def forward(value):
    def target(place, block):
        half = half_of(lax.axis_size("blk"))
        return place ^ (2 if block % half == half - 1 else 0), block + 1

    return move(value, target)


def backward(value):
    def target(place, block):
        half = half_of(lax.axis_size("blk"))
        return place ^ (2 if block % half == 0 else 0), block - 1

    return move(value, target)


def back_two(value):
    def target(place, block):
        half = half_of(lax.axis_size("blk"))
        return place ^ (2 if block % half < 2 else 0), block - 2

    return move(value, target)


def around_first(value):
    return move(value, lambda place, block: (place, turn(block, -1)))


def around_second(value):
    def target(place, block):
        half = half_of(lax.axis_size("blk"))
        source = turn(block, 1)
        return place ^ (2 if source % half >= half - 2 else 0), source + 2

    return move(value, target)


def call(kernel, operands, shapes, micros, far=(), tokens=(), scalars=(), scratch=(), direct=False, flag=False):
    whole = pl.BlockSpec(memory_space=pltpu.VMEM)
    anywhere = pl.BlockSpec(memory_space=pl.ANY)
    hbm = pl.BlockSpec(memory_space=pltpu.HBM)
    in_specs = [pl.BlockSpec(memory_space=pltpu.SMEM)] * len(scalars) + [whole] * len(operands)
    return pl.pallas_call(
        kernel,
        out_shape=[jax.ShapeDtypeStruct(s, d) for s, d in list(shapes) + [FLAG] * flag],
        in_specs=in_specs + [hbm] * len(far) + [anywhere] * len(tokens),
        out_specs=[hbm if direct else whole] * len(shapes) + [whole] * flag,
        scratch_shapes=list(scratch),
        compiler_params=pltpu.CompilerParams(vmem_limit_bytes=VMEM_LIMIT),
        cost_estimate=pl.CostEstimate(
            flops=int(micros * 1000000000), bytes_accessed=0, transcendentals=0
        ),
    )(*[v[None] for v in scalars], *operands, *far, *tokens)


def after(value, *tokens, micros=0):
    anywhere = pl.BlockSpec(memory_space=pl.ANY)
    return pl.pallas_call(
        lambda *refs: None,
        out_shape=jax.ShapeDtypeStruct(value.shape, value.dtype),
        in_specs=[anywhere] * (1 + len(tokens)),
        out_specs=anywhere,
        input_output_aliases={0: 0},
        compiler_params=pltpu.CompilerParams(vmem_limit_bytes=TIE_LIMIT),
        cost_estimate=pl.CostEstimate(
            flops=int(micros * 10**9), bytes_accessed=0, transcendentals=0
        ),
    )(value, *tokens)


def fetch(sources, targets, sems):
    copies = [
        pltpu.make_async_copy(source, target, sems.at[i])
        for i, (source, target) in enumerate(zip(sources, targets))
    ]
    for copy in copies:
        copy.start()
    return copies


def middle(pre_gate, pre_up, hidden_grad):
    sigmoid_gate = jax.nn.sigmoid(pre_gate)
    active = pre_gate * sigmoid_gate
    hidden = (active * pre_up).astype(jnp.bfloat16)
    gate_delta = (
        hidden_grad * pre_up * sigmoid_gate * (1.0 + pre_gate * (1.0 - sigmoid_gate))
    ).astype(jnp.bfloat16)
    up_delta = (hidden_grad * active).astype(jnp.bfloat16)
    return hidden, jnp.concatenate([gate_delta, up_delta], axis=1)


def columns(place, part, k, start, size):
    return pl.ds(pl.multiple_of((place ^ k) * part + start, 128), size)


def write_terms(place, part, units, hidden, delta, normed, cot, send, keep):
    size = part // PIECES
    for k in (1, 3, 0, 2):
        for side in range(PIECES):
            at = columns(place, part, k, side * size, size)
            start = k // 2 * part + side * size
            out = keep
            if k % 2:
                out = send[start // (2 * size)]
                start = start % (2 * size)
            into = slice(start, start + size)
            out[:2 * units, into] = mul(delta, normed[:, at], TN).astype(out.dtype)
            out[2 * units:, into] = mul(hidden, cot[:, at], TN).astype(out.dtype)


def pack_kernel(part, units, place_ref, place_1, place_2, gate, up, down, *rest):
    outs, (gates, ups, downs, sems) = rest[:2], rest[2:]
    place = place_ref[0]
    sources, targets = [], []
    for i, k in enumerate((0, 2)):
        at = columns(place, part, k, 0, part)
        sources += [gate.at[at, :], up.at[at, :], down.at[:, at]]
        targets += [gates.at[i], ups.at[i], downs.at[i]]
    copies = fetch(sources, targets, sems)
    for i, out in enumerate(outs):
        for copy in copies[3 * i:3 * i + 3]:
            copy.wait()
        out[:, :units] = gates[i]
        out[:, units:2 * units] = ups[i]
        out[:, 2 * units:] = jnp.transpose(downs[i])


def own_kernel(gain, tokens_far, cot_far, gate_far, up_far, down_far, *rest):
    cot, normed, inverse_ref, hidden_ref, delta_ref, tokens, gate, up, down, sems = rest[-10:]
    copies = fetch(
        (tokens_far, cot_far, gate_far, up_far, down_far), (tokens, cot, gate, up, down), sems
    )
    copies[0].wait()

    def strip(i, carry):
        rows = pl.ds(pl.multiple_of(i * STRIP, STRIP), STRIP)
        wide = tokens[rows, :].astype(jnp.float32)
        inverse = lax.rsqrt(jnp.mean(wide * wide, axis=-1, keepdims=True) + epsilon)
        inverse_ref[rows, :] = inverse
        normed[rows, :] = (wide * inverse * gain[...]).astype(jnp.bfloat16)
        return carry

    lax.fori_loop(0, tokens.shape[0] // STRIP, strip, 0)
    for copy in copies[1:]:
        copy.wait()
    hidden, delta = middle(
        mul(normed[...], gate[...]), mul(normed[...], up[...]), mul(cot[...], down[...], NT)
    )
    hidden_ref[...] = hidden
    delta_ref[...] = delta


def terms_kernel(part, units, place_ref, normed, cot, hidden, delta, *rest):
    write_terms(
        place_ref[0], part, units, hidden[...], delta[...], normed, cot, rest[-PIECES - 1:-1], rest[-1]
    )


def shard_kernel(part, units, layout, place_ref, normed, cot, *rest):
    pieces = rest[:len(layout)]
    hidden_ref, delta_ref = rest[-PIECES - 3:-PIECES - 1]
    send, keep = rest[-PIECES - 1:-1], rest[-1]
    place = place_ref[0]
    pre = None
    grad = None
    for (k, start, size), piece in zip(layout, pieces):
        at = columns(place, part, k, start, size)
        pre_here = mul(normed[:, at], piece[:, :2 * units])
        grad_here = mul(cot[:, at], piece[:, 2 * units:])
        pre = pre_here if pre is None else pre + pre_here
        grad = grad_here if grad is None else grad + grad_here
    hidden, delta = middle(pre[:, :units], pre[:, units:], grad)
    hidden_ref[...] = hidden
    delta_ref[...] = delta
    write_terms(place, part, units, hidden, delta, normed, cot, send, keep)


def summed(part, keep, arrived):
    size = 2 * part // PIECES
    total = [
        keep[:, i * size:(i + 1) * size] + arrived[i][...].astype(jnp.float32)
        for i in range(PIECES)
    ]
    return jnp.concatenate(total, axis=1)


def add_kernel(part, keep, *rest):
    total = summed(part, keep, rest[:PIECES])
    out, mine = rest[-2:]
    mine[...] = total[:, :part]
    out[...] = total[:, part:].astype(jnp.bfloat16)


def split_add_kernel(part, keep, *rest):
    half = part // 2
    total = summed(part, keep, rest[:PIECES])
    low, high, mine = rest[-3:]
    mine[...] = total[:, :part]
    low[...] = total[:, part:part + half].astype(jnp.bfloat16)
    high[...] = total[:, part + half:].astype(jnp.bfloat16)


def last_add_kernel(part, keep, mine_1, here_1, *rest):
    half = part // 2
    total = summed(part, keep, rest[:PIECES])
    low, high, mine, near = rest[-4:]
    mine[...] = total[:, :part]
    low[...] = total[:, part:part + half].astype(jnp.bfloat16)
    high[...] = total[:, part + half:].astype(jnp.bfloat16)
    near[...] = (mine_1[...] + here_1[...].astype(jnp.float32)).astype(jnp.bfloat16)


def hop_kernel(start, mine, arrived, *rest):
    size = arrived.shape[1]
    total = mine[:, start:start + size] + arrived[...].astype(jnp.float32)
    if start == 0:
        later, out, later_out = rest[0], rest[-2], rest[-1]
        later_out[...] = later[...]
    else:
        out = rest[-1]
    out[...] = total.astype(jnp.bfloat16)


def final_kernel(units, mine, here_low, here_high, near, low, high, gate, up, down, keep_g, keep_u, keep_d, sems):
    half = low.shape[1]
    for start, here, last in ((0, here_low, low), (half, here_high, high)):
        at = slice(start, start + half)
        total = mine[:, at] + here[...].astype(jnp.float32) + near[:, at].astype(jnp.float32)
        total = (total + last[...].astype(jnp.float32)) * grad_scale
        keep_g[at, :] = jnp.transpose(total[:units])
        keep_u[at, :] = jnp.transpose(total[units:2 * units])
        keep_d[:, at] = total[2 * units:]
    for copy in fetch((keep_g, keep_u, keep_d), (gate, up, down), sems):
        copy.wait()


def strips(rows, kept, far, sems, body):
    group = rows // DP
    copies = []
    for g in range(DP):
        def strip(i, carry):
            body(pl.ds(pl.multiple_of(g * group + i * STRIP, STRIP), STRIP))
            return carry

        lax.fori_loop(0, group // STRIP, strip, 0)
        here = pl.ds(g * group, group)
        copies.append(pltpu.make_async_copy(kept.at[here, :], far.at[here, :], sems.at[g]))
        copies[-1].start()
    for copy in copies:
        copy.wait()


def forward_out_kernel(part, units, layouts, place_1, place_2, hidden_0, hidden_1, hidden_2, *rest):
    count = len(layouts[0]) + len(layouts[1])
    pieces, rest = rest[:count], rest[count:]
    tokens_far, down_far = rest[:2]
    block_out, flag, tokens, down, mlp, kept, in_sems, out_sems = rest[-8:]
    flag[...] = jnp.zeros_like(flag)
    copies = fetch((down_far, tokens_far), (down, tokens), in_sems)
    copies[0].wait()
    for j in range(DP):
        at = pl.ds(j * part, part)
        mlp[:, at] = mul(hidden_0[...], down[:, at])
    used = 0
    for place_ref, layout, hidden in ((place_1, layouts[0], hidden_1), (place_2, layouts[1], hidden_2)):
        place = place_ref[0]
        for k, start, size in layout:
            at = columns(place, part, k, start, size)
            mlp[:, at] += mul(hidden[...], pieces[used][:, 2 * units:], NT)
            used += 1
    copies[1].wait()

    def body(rows):
        kept[rows, :] = (tokens[rows, :].astype(jnp.float32) + mlp[rows, :]).astype(jnp.bfloat16)

    strips(tokens.shape[0], kept, block_out, out_sems, body)


def backward_out_kernel(part, units, layouts, place_1, place_2, cot, gain, inverse_ref, delta_0, delta_1, delta_2, *rest):
    count = len(layouts[0]) + len(layouts[1])
    pieces, rest = rest[:count], rest[count:]
    tokens_far, gate_far, up_far, input_grad, flag, tokens, gate, up, dnormed, kept, in_sems, out_sems = rest
    flag[...] = jnp.zeros_like(flag)
    copies = fetch((gate_far, up_far, tokens_far), (gate, up, tokens), in_sems)
    for copy in copies[:2]:
        copy.wait()
    for j in range(DP):
        at = pl.ds(j * part, part)
        dnormed[:, at] = mul(delta_0[:, :units], gate[at, :], NT) + mul(
            delta_0[:, units:], up[at, :], NT
        )
    used = 0
    for place_ref, layout, delta in ((place_1, layouts[0], delta_1), (place_2, layouts[1], delta_2)):
        place = place_ref[0]
        for k, start, size in layout:
            at = columns(place, part, k, start, size)
            dnormed[:, at] += mul(delta[...], pieces[used][:, :2 * units], NT)
            used += 1
    copies[2].wait()

    def body(rows):
        wide = tokens[rows, :].astype(jnp.float32)
        inverse = inverse_ref[rows, :]
        scaled = wide * inverse
        along = dnormed[rows, :] * gain[...]
        norm_back = inverse * (along - scaled * jnp.mean(along * scaled, axis=-1, keepdims=True))
        kept[rows, :] = (cot[rows, :].astype(jnp.float32) + norm_back).astype(jnp.bfloat16)

    strips(tokens.shape[0], kept, input_grad, out_sems, body)


def shards(tokens, cotangent, norm_gain, gate_weight, up_weight, down_weight):
    place = lax.axis_index("dp")
    block = lax.axis_index("blk")
    span = half_of(lax.axis_size("blk"))
    rows, model = tokens.shape
    part = model // DP
    half = part // 2
    units = gate_weight.shape[1]
    width = 3 * units
    bf16, f32 = jnp.bfloat16, jnp.float32
    place_1 = place ^ jnp.where(block % span < 1, 2, 0)
    place_2 = place ^ jnp.where(block % span < 2, 2, 0)
    gate_weight, up_weight, down_weight, tokens = (
        pltpu.with_memory_space_constraint(v, pltpu.HBM)
        for v in (gate_weight, up_weight, down_weight, tokens)
    )
    weights = [gate_weight, up_weight, down_weight]
    gain = norm_gain[None, :]
    dma = pltpu.SemaphoreType.DMA

    piece, other = call(
        functools.partial(pack_kernel, part, units), [], [((part, width), bf16)] * 2, 2,
        far=weights, scalars=(place, place_1, place_2),
        scratch=[pltpu.VMEM((2, part, units), bf16)] * 2
        + [pltpu.VMEM((2, units, part), bf16), dma((6,))],
    )
    one = forward(piece)
    two_z = around_first(other)

    acts = [((rows, units), bf16), ((rows, 2 * units), bf16)]
    terms = [((width, 2 * part // PIECES), bf16)] * PIECES + [((width, 2 * part), f32)]

    cot, normed, inverse, hidden_0, delta_0 = call(
        own_kernel, [gain], [((rows, model), bf16)] * 2 + [((rows, 1), f32)] + acts, 5,
        far=[tokens, cotangent] + weights, tokens=(other,),
        scratch=[pltpu.VMEM((rows, model), bf16)] + [pltpu.VMEM((model, units), bf16)] * 2
        + [pltpu.VMEM((units, model), bf16), dma((5,))],
    )

    *send, keep = call(
        functools.partial(terms_kernel, part, units), [normed, cot, hidden_0, delta_0], terms, 5,
        scalars=(place,),
    )
    def add(keep, send, tokens=()):
        return call(
            functools.partial(add_kernel, part), [keep] + [swap(v, 1) for v in send],
            [((width, part), bf16), ((width, part), f32)], 1, tokens=tokens,
        )

    low_0, high_0, mine_0 = call(
        functools.partial(split_add_kernel, part), [keep] + [swap(v, 1) for v in send],
        [((width, half), bf16)] * 2 + [((width, part), f32)], 1,
    )
    here_low = swap(low_0, 2)
    one = after(one, low_0, two_z)
    one_x = swap(one, 2)
    two = forward(one)
    two_z = around_second(two_z)
    ones = [one, one_x, swap(one, 1), swap(one_x, 1)]
    twos = [two, two_z, swap(two, 1), swap(two_z, 1)]
    layout = [(k, 0, part) for k in (0, 2, 1, 3)]

    hidden_1, delta_1, *send, keep = call(
        functools.partial(shard_kernel, part, units, layout), [normed, cot] + ones,
        acts + terms, 4, scalars=(place_1,), tokens=(low_0, two, two_z),
    )
    keep_1, send_1 = keep, send

    hidden_2, delta_2, *send, keep = call(
        functools.partial(shard_kernel, part, units, layout), [normed, cot] + twos,
        acts + terms, 4, scalars=(place_2,), tokens=(hidden_1,),
    )
    input_grad, flag_backward = call(
        functools.partial(backward_out_kernel, part, units, (layout, layout)),
        [cot, gain, inverse, delta_0, delta_1, delta_2] + ones + twos,
        [((rows, model), bf16)], 5,
        far=[tokens, gate_weight, up_weight], scalars=(place_1, place_2), direct=True, flag=True,
        scratch=[
            pltpu.VMEM((rows, model), bf16), pltpu.VMEM((model, units), bf16),
            pltpu.VMEM((model, units), bf16), pltpu.VMEM((rows, model), f32),
            pltpu.VMEM((rows, model), bf16), dma((3,)), dma((DP,)),
        ],
    )

    here_low = after(here_low, hidden_1, micros=14)
    out_1, mine_1 = add(keep_1, send_1, (here_low,))
    here_1 = swap(out_1, 2)
    low_2, high_2, mine_2, near = call(
        functools.partial(last_add_kernel, part),
        [keep, mine_1, here_1] + [swap(v, 1) for v in send],
        [((width, half), bf16)] * 2 + [((width, part), f32), ((width, part), bf16)], 1,
        tokens=(flag_backward,),
    )
    near = after(backward(near), micros=8)

    block_out, flag_forward = call(
        functools.partial(forward_out_kernel, part, units, (layout, layout)),
        [hidden_0, hidden_1, hidden_2] + ones + twos, [((rows, model), bf16)], 4,
        far=[tokens, down_weight], tokens=(low_2,), scalars=(place_1, place_2), direct=True, flag=True,
        scratch=[
            pltpu.VMEM((rows, model), bf16), pltpu.VMEM((units, model), bf16),
            pltpu.VMEM((rows, model), f32), pltpu.VMEM((rows, model), bf16), dma((2,)), dma((DP,)),
        ],
    )
    sum_low, high_2 = call(
        functools.partial(hop_kernel, 0), [mine_2, swap(low_2, 2), high_2],
        [((width, half), bf16)] * 2, 0.5, tokens=(flag_forward,),
    )
    sum_low = back_two(sum_low)
    sum_high, = call(
        functools.partial(hop_kernel, half), [mine_2, swap(high_2, 2)],
        [((width, half), bf16)], 0.5,
    )
    here_high = swap(after(high_0, sum_high), 2)
    sum_high = back_two(sum_high)

    gate_grad, up_grad, down_grad = call(
        functools.partial(final_kernel, units), [mine_0, here_low, here_high, near, sum_low, sum_high],
        [((part, units), f32)] * 2 + [((units, part), f32)], 2, direct=True,
        scratch=[pltpu.VMEM((part, units), f32)] * 2 + [pltpu.VMEM((units, part), f32), dma((3,))],
    )
    return block_out, input_grad, gate_grad, up_grad, down_grad


def solution(mesh):
    in_specs = (
        P(("dp", "blk"), None),
        P(("dp", "blk"), None),
        P(),
        P(None, "blk"),
        P(None, "blk"),
        P("blk", None),
    )
    out_specs = (
        P(("dp", "blk"), None),
        P(("dp", "blk"), None),
        P("dp", "blk"),
        P("dp", "blk"),
        P("blk", "dp"),
    )
    return jax.shard_map(shards, mesh=mesh, in_specs=in_specs, out_specs=out_specs, check_vma=False)
```
